32 devices in a mesh: groups: 2 (over y), neuron: 4 (over z), req: 4 (over x, core).
Axes of the slice: x: 2, y: 2, z: 4, core: 2. Of those that a mesh axis runs over, the one named last changes fastest.
Arguments:
- hidden0: bfloat16 [32, 8, 6144], P(('groups', 'neuron', 'req')), parts along dimension 0, may hold values from -6 to 6
- embeds: bfloat16 [2, 32, 8, 6144], P(None, ('groups', 'neuron', 'req')), parts along dimension 1, may hold values from -6 to 6
- parents: int32 [2, 32, 8], P(None, ('groups', 'neuron', 'req')), parts along dimension 1, may hold values from 0 to 7
- active: int32 [2, 32, 8, 38], P(None, ('groups', 'neuron', 'req')), parts along dimension 1, may hold values from 0 to 383, as said below
- verify_row: int32 [32], P(('groups', 'neuron', 'req')), parts along dimension 0, may hold values from 0 to 7
- norm_gain: float32 [6144], replicated, may hold values from 0.5 to 1.5
- norm_shift: float32 [6144], replicated, may hold values from -3 to 3
- weight_in: bfloat16 [6144, 49152], P(None, ('neuron', 'req')), may hold values from -0.078125 to 0.078125
- bias_in: float32 [49152], P(('neuron', 'req')), may hold values from -4 to 4
- weight_out: bfloat16 [49152, 6144], P(('neuron', 'req')), may hold values from -0.078125 to 0.078125
- bias_out: float32 [6144], replicated, may hold values from -4 to 4
Outputs:
- draft: bfloat16 [32, 8, 6144], P(('groups', 'neuron', 'req')), parts along dimension 0
- verified: bfloat16 [32, 6144], P(('groups', 'neuron', 'req')), parts along dimension 0
The draws below stay inside these ranges and needn't reach their ends.
There are 2 independent parts, one for each index of `groups`. The reference program is written for one: setup_inputs(seed, part) draws one part's arguments, and reference() takes and returns one part's arrays. A program takes and returns all parts, laid end to end along the dimension named above; an argument that names none is the same for every part. Nothing has to cross between parts.
Inputs may be any that keep to these rules, and one draw needn't show every extreme that they name: For each depth, a row's 38 entries are distinct block numbers. Take the 8 rows held by one device. For every device i, the neuron blocks that device i holds (numbers i * 24 to (i + 1) * 24 - 1) appear in the active lists of at most 8 of those rows, and some device i reaches exactly 8.
All inputs are finite; a program needn't handle non-finite values.
Results may differ from the reference program's by a relative error of at most 0.0055.
Values may be sent and summed in bfloat16 or wider, within the bound.
A program may use at most 192 MiB of HBM per device.

```python
import jax
import jax.numpy as jnp
from jax import lax

D = 6144
FF = 49152
NBLK = 384
BS = 128
NACT = 38
FRONT = 8
REQ_DEV = 1
DEPTHS = 2
SHARDS = 16
BLK_DEV = 24
REQS = 16
ROWS_DEV = 8
ROUNDS = 19


def shuffled(order_key):
    return jax.random.permutation(order_key, SHARDS)


def draw_active(key, part):
    key = jax.random.fold_in(key, 7)
    group_total = DEPTHS * SHARDS
    picks = ROWS_DEV * NACT
    order_keys = jax.random.split(jax.random.fold_in(key, 1), group_total * ROUNDS)
    orders = jax.vmap(shuffled)(order_keys).reshape(group_total, ROUNDS * SHARDS)[:, :picks]
    devices = orders.reshape(group_total, ROWS_DEV, NACT).astype(jnp.int32)
    offsets = jax.random.randint(jax.random.fold_in(key, 2), (group_total, ROWS_DEV, SHARDS), 0, BLK_DEV).astype(jnp.int32)
    base = jnp.take_along_axis(offsets, devices, axis=2)
    round_of = (jnp.arange(picks, dtype=jnp.int32) // SHARDS).reshape(1, ROWS_DEV, NACT)
    blocks = devices * BLK_DEV + (base + round_of) % BLK_DEV
    return blocks.reshape(DEPTHS, SHARDS * REQ_DEV, FRONT, NACT).astype(jnp.int32)


def touch_ends(entries, rng, low, top_value):
    longest = entries.shape.index(max(entries.shape))
    spots = []
    for shift in (0, 1):
        where = [jax.random.randint(jax.random.fold_in(rng, axis), (), 0, length) for axis, length in enumerate(entries.shape)]
        where[longest] = (where[longest] + shift) % entries.shape[longest]
        spots.append(tuple(where))
    return entries.at[spots[0]].set(low).at[spots[1]].set(top_value)


def level_of(key, extent, cuts, smallest, largest):
    gain = 1.0
    for dim, shards_of in cuts:
        steps = jax.random.uniform(jax.random.fold_in(jax.random.fold_in(key, 6), dim), (shards_of,), jnp.float32, smallest / len(cuts), largest / len(cuts))
        gain = gain * jnp.repeat(jnp.exp(steps), extent[dim] // shards_of).reshape((-1,) + (1,) * (len(extent) - 1 - dim))
    return gain


def gaussian(rng, extent, width, limit, cuts=(), held_as=jnp.bfloat16):
    entries = jax.random.normal(rng, extent, jnp.float32) * width
    if len(cuts) > 0:
        entries = level_of(rng, extent, cuts, -0.22, 0.18) * entries
    return jnp.clip(entries, min=-limit, max=limit).astype(held_as)


def setup_inputs(seed: int = 0, part: int = 0) -> dict:
    key_list = jax.random.split(jax.random.key(seed), 12)
    part_splits = jax.random.split(jax.random.fold_in(key_list[11], part), 12)
    hidden0 = gaussian(part_splits[0], (REQS, FRONT, D), 1.0, 6.0, ((0, 16),))
    embeds = gaussian(part_splits[1], (DEPTHS, REQS, FRONT, D), 1.0, 6.0, ((1, 16),))
    parents = touch_ends(jax.random.randint(part_splits[2], (DEPTHS, REQS, FRONT), 0, FRONT), jax.random.fold_in(part_splits[2], 1), 0, FRONT - 1).astype(jnp.int32)
    active = draw_active(jax.random.fold_in(jax.random.fold_in(key_list[11], part), 71), part)
    verify_row = touch_ends(jax.random.randint(part_splits[4], (REQS,), 0, FRONT), jax.random.fold_in(part_splits[4], 1), 0, FRONT - 1).astype(jnp.int32)
    norm_gain = jnp.clip(1.0 + 0.1 * jax.random.normal(key_list[5], (D,), jnp.float32), 0.5, 1.5)
    norm_shift = gaussian(key_list[6], (D,), 0.3, 3.0, (), jnp.float32)
    weight_in = gaussian(key_list[7], (D, FF), D ** -0.5, 0.078125, ((1, 16),))
    bias_in = gaussian(key_list[8], (FF,), 0.5, 4.0, ((0, 16),), jnp.float32)
    weight_out = gaussian(key_list[9], (FF, D), (NACT * BS) ** -0.5, 0.078125, ((0, 16),))
    bias_out = gaussian(key_list[10], (D,), 0.5, 4.0, (), jnp.float32)
    return dict(hidden0=hidden0, embeds=embeds, parents=parents, active=active, verify_row=verify_row, norm_gain=norm_gain, norm_shift=norm_shift, weight_in=weight_in, bias_in=bias_in, weight_out=weight_out, bias_out=bias_out)


norm_eps = 1e-05

def normalize(values, norm_gain, norm_shift):
    row_mean = lax.optimization_barrier(jnp.mean(values, axis=-1, keepdims=True))
    centered = values - row_mean
    row_var = lax.optimization_barrier(jnp.mean(centered * centered, axis=-1, keepdims=True))
    return (centered * lax.rsqrt(row_var + norm_eps) * norm_gain + norm_shift).astype(jnp.bfloat16)

def reference(hidden0, embeds, parents, active, verify_row, norm_gain, norm_shift, weight_in, bias_in, weight_out, bias_out):
    row_total = REQS * FRONT
    group_width = BLK_DEV * BS
    states = hidden0.astype(jnp.float32)
    for depth_step in range(DEPTHS):
        picked = jnp.take_along_axis(states, parents[depth_step][:, :, None], axis=1)
        pre_state = picked + embeds[depth_step].astype(jnp.float32)
        normed = normalize(pre_state, norm_gain, norm_shift)
        flat_rows = normed.reshape(row_total, D)
        block_list = active[depth_step].reshape(row_total, NACT)
        member = jnp.any(block_list[:, :, None] == jnp.arange(NBLK, dtype=jnp.int32)[None, None, :], axis=1).astype(jnp.float32)

        def add_group(total, group):
            first = group * group_width
            columns = lax.dynamic_slice_in_dim(weight_in, first, group_width, 1)
            bias_part = lax.dynamic_slice_in_dim(bias_in, first, group_width, 0)
            block_mask = lax.dynamic_slice_in_dim(member, group * BLK_DEV, BLK_DEV, 1)
            preact = jnp.dot(flat_rows, columns, preferred_element_type=jnp.float32) + bias_part
            hidden = (jax.nn.relu(preact).reshape(row_total, BLK_DEV, BS) * block_mask[:, :, None]).reshape(row_total, group_width).astype(jnp.bfloat16)
            rows_out = lax.dynamic_slice_in_dim(weight_out, first, group_width, 0)
            partial_value = jnp.dot(hidden, rows_out, preferred_element_type=jnp.float32).astype(jnp.bfloat16)
            partial_value = lax.optimization_barrier(partial_value)
            return (total + partial_value.astype(jnp.float32), None)
        total, unused = lax.scan(add_group, jnp.zeros((row_total, D), jnp.float32), jnp.arange(SHARDS, dtype=jnp.int32))
        states = pre_state + (total + bias_out).reshape(REQS, FRONT, D)
    verify_in = jnp.take_along_axis(normed, verify_row[:, None, None], axis=1)[:, 0]
    verify_base = jnp.take_along_axis(pre_state, verify_row[:, None, None], axis=1)[:, 0]
    verify_hidden = jax.nn.relu(jnp.dot(verify_in, weight_in, preferred_element_type=jnp.float32) + bias_in).astype(jnp.bfloat16)
    dense_sum = jnp.dot(verify_hidden, weight_out, preferred_element_type=jnp.float32)
    verified = (verify_base + bias_out + dense_sum).astype(jnp.bfloat16)
    return (states.astype(jnp.bfloat16), verified)
```

```python
import functools

import jax
import jax.numpy as jnp
from jax import lax
from jax.experimental import pallas as pl
from jax.experimental.pallas import tpu as pltpu
from jax.sharding import PartitionSpec as P

BS = 128
DEPTHS = 2
CORES = 2
CHUNK = 1024
SUB = CHUNK // 2
SLOTS = 4
ROWS = 8
VMEM_LIMIT = 63 * 1024 * 1024

norm_eps = 1e-05
MESH = pl.DeviceIdType.MESH
F32 = jnp.float32
BF16 = jnp.bfloat16


def kernel(
    nz,
    nx,
    hidden_ref,
    embeds_ref,
    parents_ref,
    active_ref,
    vrow_ref,
    gain_ref,
    shift_ref,
    win_hbm,
    bin_ref,
    wout_hbm,
    bout_ref,
    draft_ref,
    verified_ref,
    win_v,
    wout_v,
    xbuf,
    mbuf,
    mask_v,
    flag_v,
    hid,
    ybuf,
    rc,
    rx,
    rz,
    pre_v,
    state_v,
    ver_v,
    vline,
    win_sem,
    wout_sem,
    ag_recv,
    ag_zs,
    ag_xs,
    ag_cs,
    rc_send,
    rc_recv,
    rx_send,
    rx_recv,
    rz_send,
    rz_recv,
):
    shards = CORES * nx * nz
    features = hidden_ref.shape[2]
    half = features // 2
    tiles, _, ht = win_v.shape
    nblk = mask_v.shape[1]
    blk_tile = ht // BS
    chunks = features // CHUNK
    outs_dev = features // SUB
    all_rows = shards * ROWS

    g = lax.axis_index("groups")
    z = lax.axis_index("neuron")
    req = lax.axis_index("req")
    x = req // CORES
    c = req % CORES
    me = z * (nx * CORES) + req
    oc = 1 - c

    def dev(zz, xx, cc):
        return (g, zz, xx * CORES + cc)

    def zpeer(d):
        out, bit = z, 1
        while bit < nz:
            if d & bit:
                out = out + bit - 2 * bit * ((z // bit) % 2)
            bit *= 2
        return out

    zs = [zpeer(d) for d in range(nz)]
    xs = [(x + e) % nx for e in range(nx)]

    barrier = pltpu.get_barrier_semaphore()
    peers = [dev(zs[d], x, c) for d in range(1, nz)]
    peers += [dev(z, xs[e], c) for e in range(1, nx)]
    peers += [dev(z, x, oc)]
    for peer in peers:
        pl.semaphore_signal(barrier, inc=1, device_id=peer, device_id_type=MESH)

    def win_copy(t):
        return pltpu.make_async_copy(
            win_hbm.at[:, pl.ds(pl.multiple_of(t * ht, ht), ht)], win_v.at[t], win_sem.at[t]
        )

    def wout_copy(k):
        col = pl.multiple_of((k % outs_dev) * SUB, SUB)
        slot = k % SLOTS
        return pltpu.make_async_copy(
            wout_hbm.at[:, pl.ds(col, SUB)], wout_v.at[slot], wout_sem.at[slot]
        )

    for t in range(tiles):
        win_copy(t).start()
    for k in range(SLOTS):
        wout_copy(k).start()

    block_ids = lax.broadcasted_iota(jnp.int32, (ROWS, nblk), 1)
    row_ids = lax.broadcasted_iota(jnp.int32, (ROWS, BS), 0)
    flag = (row_ids == vrow_ref[...]).astype(F32)
    sides = []
    for depth in range(DEPTHS):
        listed = active_ref[depth, 0]
        member = jnp.zeros((ROWS, nblk), F32)
        for j in range(listed.shape[1]):
            member = jnp.where(listed[:, j : j + 1] == block_ids, 1.0, member)
        sides.append(jnp.concatenate([member, flag], axis=1))
    mbuf[c, x, z] = jnp.concatenate(sides, axis=0).astype(BF16)

    def prepare(depth):
        states = hidden_ref[0].astype(F32) if depth == 0 else state_v[...]
        eye_r = lax.broadcasted_iota(jnp.int32, (ROWS, ROWS), 0)
        eye_c = lax.broadcasted_iota(jnp.int32, (ROWS, ROWS), 1)
        par = jnp.sum(
            jnp.where(eye_r == eye_c, jnp.broadcast_to(parents_ref[depth], (ROWS, ROWS)), 0),
            axis=1,
            keepdims=True,
        )
        picked = jnp.zeros((ROWS, features), F32)
        for p in range(ROWS):
            picked = jnp.where(par == p, states[p : p + 1, :], picked)
        pre = picked + embeds_ref[depth, 0].astype(F32)
        pre_v[...] = pre
        centered = pre - jnp.mean(pre, axis=-1, keepdims=True)
        var = jnp.mean(centered * centered, axis=-1, keepdims=True)
        normed = centered * lax.rsqrt(var + norm_eps) * gain_ref[...] + shift_ref[...]
        xbuf[c, x, z] = jnp.concatenate([normed[:, :half], normed[:, half:]], axis=0).astype(BF16)

    def gather(bufs):
        started = []

        def send(i, block, to, send_sem):
            cc, xx, zz = block
            ref = bufs[i][1].at[cc, xx, zz]
            copy = pltpu.make_async_remote_copy(
                src_ref=ref,
                dst_ref=ref,
                send_sem=send_sem,
                recv_sem=ag_recv.at[bufs[i][0], cc, xx, zz],
                device_id=to,
                device_id_type=MESH,
            )
            copy.start()
            started.append(copy)

        def arrived(i, block):
            cc, xx, zz = block
            ref = bufs[i][1].at[cc, xx, zz]
            pltpu.make_async_copy(ref, ref, ag_recv.at[bufs[i][0], cc, xx, zz]).wait()

        many = range(len(bufs))
        for i in many:
            b = bufs[i][0]
            for d in range(1, nz):
                send(i, (c, x, z), dev(zs[d], x, c), ag_zs.at[b, d])
        for d in range(nz):
            for i in many:
                b = bufs[i][0]
                if d > 0:
                    arrived(i, (c, x, zs[d]))
                for e in range(1, nx):
                    send(i, (c, x, zs[d]), dev(z, xs[e], c), ag_xs.at[b, e, d])
                send(i, (c, x, zs[d]), dev(z, x, oc), ag_cs.at[b, 0, d])
        for d in range(nz):
            for e in range(1, nx):
                for i in many:
                    b = bufs[i][0]
                    arrived(i, (c, xs[e], zs[d]))
                    send(i, (c, xs[e], zs[d]), dev(z, x, oc), ag_cs.at[b, e, d])
        for e in range(nx):
            for d in range(nz):
                for i in many:
                    arrived(i, (oc, xs[e], zs[d]))
        for copy in started:
            copy.wait_send()

    def swap_rows():
        @pl.loop(0, CORES * nx)
        def _(i):
            cc, xx = i // nx, i % nx
            for zz in range(0, nz, 2):
                first = xbuf[cc, xx, zz].astype(F32)
                second = xbuf[cc, xx, zz + 1].astype(F32)
                xbuf[cc, xx, zz] = jnp.concatenate([first[:ROWS], second[:ROWS]], axis=0).astype(BF16)
                xbuf[cc, xx, zz + 1] = jnp.concatenate([first[ROWS:], second[ROWS:]], axis=0).astype(BF16)

    def first_projection(depth):
        meta = mbuf[...].astype(F32).reshape(shards, DEPTHS * ROWS, nblk + BS)
        meta = meta[:, depth * ROWS : (depth + 1) * ROWS, :].reshape(all_rows, nblk + BS)
        mask_v[...] = meta[:, :nblk].astype(BF16)
        if depth == DEPTHS - 1:
            flag_v[...] = meta[:, nblk:]

        @pl.loop(0, tiles)
        def _(t):
            if depth == 0:
                win_copy(t).wait()
            pairs = xbuf.reshape(shards // 2, 2, 2 * ROWS, half)
            pre = jnp.dot(
                pairs[:, 0].reshape(all_rows, half), win_v[t, :half, :], preferred_element_type=F32
            )
            pre += jnp.dot(
                pairs[:, 1].reshape(all_rows, half), win_v[t, half:, :], preferred_element_type=F32
            )
            col = pl.ds(pl.multiple_of(t * ht, ht), ht)
            act = jnp.maximum(pre + bin_ref[:, col], 0.0)
            which = lax.broadcasted_iota(jnp.int32, (nblk, ht), 0)
            unit = lax.broadcasted_iota(jnp.int32, (nblk, ht), 1) // BS
            spread = (which == unit + (me * tiles + t) * blk_tile).astype(F32).astype(BF16)
            keep = jnp.dot(mask_v[...], spread, preferred_element_type=F32)
            hid[:all_rows, col] = (act * keep).astype(BF16)
            if depth == DEPTHS - 1:
                wide = jnp.concatenate([flag_v[...]] * blk_tile, axis=1)
                one = jnp.sum((act * wide).reshape(shards, ROWS, ht), axis=1)
                hid[all_rows:, col] = one.astype(BF16)

    def second_projection(depth):
        last = depth == DEPTHS - 1
        width = SUB + BS if last else SUB
        lanes = pl.ds(0, width)
        rows = hid.shape[0] if last else all_rows

        def core_copy(n):
            return pltpu.make_async_remote_copy(
                src_ref=ybuf.at[n, oc, :, :, :, lanes],
                dst_ref=rc.at[n, :, :, :, lanes],
                send_sem=rc_send.at[n],
                recv_sem=rc_recv.at[n],
                device_id=dev(z, x, oc),
                device_id_type=MESH,
            )

        def x_copy(n, e):
            return pltpu.make_async_remote_copy(
                src_ref=ybuf.at[n, c, xs[e], :, :, lanes],
                dst_ref=rx.at[n, e - 1, :, :, lanes],
                send_sem=rx_send.at[n, e],
                recv_sem=rx_recv.at[n, e],
                device_id=dev(z, xs[e], c),
                device_id_type=MESH,
            )

        def z_copy(n, d):
            return pltpu.make_async_remote_copy(
                src_ref=ybuf.at[n, c, x, zs[d], :, lanes],
                dst_ref=rz.at[n, d - 1, :, lanes],
                send_sem=rz_send.at[n, d],
                recv_sem=rz_recv.at[n, d],
                device_id=dev(zs[d], x, c),
                device_id_type=MESH,
            )

        def compute(n):
            slot = []
            for sub in range(2):
                k = depth * outs_dev + n * 2 + sub
                wout_copy(k).wait()
                slot.append(k % SLOTS)
            pieces = jnp.zeros((shards, ROWS, BS), F32)
            place = lax.broadcasted_iota(jnp.int32, (shards, ROWS, BS), 1)
            step = 256
            for q in range(SUB // step):
                cols = slice(q * step, (q + 1) * step)
                parts = []
                for sub in range(2):
                    y = jnp.dot(hid[:rows, :], wout_v[slot[sub], :, cols], preferred_element_type=F32)
                    parts.append(y[:all_rows].reshape(shards, ROWS, step))
                    if last:
                        for r in range(step // BS):
                            spot = (sub * SUB + q * step) // BS + r
                            line = y[all_rows : all_rows + shards, r * BS : (r + 1) * BS]
                            pieces = jnp.where(place == spot, line[:, None, :], pieces)
                packed = jnp.concatenate(parts, axis=1).astype(BF16)
                ybuf[n, :, :, :, :, cols] = packed.reshape(CORES, nx, nz, 2 * ROWS, step)
            if last:
                packed = jnp.concatenate([pieces, jnp.zeros_like(pieces)], axis=1).astype(BF16)
                ybuf[n, :, :, :, :, SUB:] = packed.reshape(CORES, nx, nz, 2 * ROWS, BS)
            core_copy(n).start()
            for sub in range(2):
                k = depth * outs_dev + n * 2 + sub + SLOTS

                @pl.when(k < DEPTHS * outs_dev)
                def _():
                    wout_copy(k).start()

        def add_core(n):
            core_copy(n).wait_recv()
            for xx in range(nx):
                total = ybuf[n, c, xx, :, :, :width].astype(F32) + rc[n, xx, :, :, :width].astype(F32)
                ybuf[n, c, xx, :, :, :width] = total.astype(BF16)
            for e in range(1, nx):
                x_copy(n, e).start()

        def add_x(n):
            total = ybuf[n, c, x, :, :, :width].astype(F32)
            for e in range(1, nx):
                x_copy(n, e).wait_recv()
                total += rx[n, e - 1, :, :, :width].astype(F32)
            ybuf[n, c, x, :, :, :width] = total.astype(BF16)
            for d in range(1, nz):
                z_copy(n, d).start()

        def add_z(n):
            total = ybuf[n, c, x, z, :, :width].astype(F32)
            for d in range(1, nz):
                z_copy(n, d).wait_recv()
                total += rz[n, d - 1, :, :width].astype(F32)
            cols = pl.ds(pl.multiple_of(n * CHUNK, CHUNK), CHUNK)
            rows_out = jnp.concatenate([total[:ROWS, :SUB], total[ROWS:, :SUB]], axis=1)
            state_v[:, cols] = pre_v[:, cols] + (rows_out + bout_ref[:, cols])
            if last:
                ver_v[n] = total[:ROWS, SUB:]

        @pl.loop(0, chunks + 3)
        def _(n):
            @pl.when(n < chunks)
            def _():
                compute(n)

            @pl.when((n >= 1) & (n < chunks + 1))
            def _():
                add_core(n - 1)

            @pl.when((n >= 2) & (n < chunks + 2))
            def _():
                add_x(n - 2)

            @pl.when(n >= 3)
            def _():
                add_z(n - 3)

        @pl.loop(0, chunks)
        def _(n):
            core_copy(n).wait_send()
            for e in range(1, nx):
                x_copy(n, e).wait_send()
            for d in range(1, nz):
                z_copy(n, d).wait_send()

    prepare(0)
    pl.semaphore_wait(barrier, len(peers))
    for depth in range(DEPTHS):
        if depth > 0:
            prepare(depth)
        gather([(0, mbuf), (1, xbuf)] if depth == 0 else [(1, xbuf)])
        swap_rows()
        first_projection(depth)
        second_projection(depth)

    draft_ref[0] = state_v[...].astype(BF16)
    full_ids = lax.broadcasted_iota(jnp.int32, (ROWS, features), 0)
    base = jnp.sum(jnp.where(full_ids == vrow_ref[...], pre_v[...], 0.0), axis=0, keepdims=True)
    for n in range(chunks):
        piece = ver_v[n]
        for r in range(ROWS):
            vline[:, n * CHUNK + r * BS : n * CHUNK + (r + 1) * BS] = piece[r : r + 1, :]
    verified_ref[...] = (base + bout_ref[...] + vline[...]).astype(BF16)


def tile_width(width, most):
    return max(t for t in range(BS, most + 1, BS) if width % t == 0)


def body(
    nz,
    nx,
    hidden0,
    embeds,
    parents,
    active,
    verify_row,
    norm_gain,
    norm_shift,
    weight_in,
    bias_in,
    weight_out,
    bias_out,
):
    features, width = weight_in.shape
    shards = CORES * nx * nz
    rows = shards * ROWS
    nblk = shards * width // BS
    ht = tile_width(width, 512)
    tiles = width // ht
    chunks = features // CHUNK
    vm = pl.BlockSpec(memory_space=pltpu.VMEM)
    hbm = pl.BlockSpec(memory_space=pl.ANY)
    dma = pltpu.SemaphoreType.DMA
    return pl.pallas_call(
        functools.partial(kernel, nz, nx),
        out_shape=(
            jax.ShapeDtypeStruct(hidden0.shape, BF16),
            jax.ShapeDtypeStruct((1, features), BF16),
        ),
        in_specs=[vm, vm, vm, vm, vm, vm, vm, hbm, vm, hbm, vm],
        out_specs=(vm, vm),
        scratch_shapes=[
            pltpu.VMEM((tiles, features, ht), BF16),
            pltpu.VMEM((SLOTS, width, SUB), BF16),
            pltpu.VMEM((CORES, nx, nz, 2 * ROWS, features // 2), BF16),
            pltpu.VMEM((CORES, nx, nz, DEPTHS * ROWS, nblk + BS), BF16),
            pltpu.VMEM((rows, nblk), BF16),
            pltpu.VMEM((rows, BS), F32),
            pltpu.VMEM((rows + shards, width), BF16),
            pltpu.VMEM((chunks, CORES, nx, nz, 2 * ROWS, SUB + BS), BF16),
            pltpu.VMEM((chunks, nx, nz, 2 * ROWS, SUB + BS), BF16),
            pltpu.VMEM((chunks, nx - 1, nz, 2 * ROWS, SUB + BS), BF16),
            pltpu.VMEM((chunks, nz - 1, 2 * ROWS, SUB + BS), BF16),
            pltpu.VMEM((ROWS, features), F32),
            pltpu.VMEM((ROWS, features), F32),
            pltpu.VMEM((chunks, ROWS, BS), F32),
            pltpu.VMEM((1, features), F32),
            dma((tiles,)),
            dma((SLOTS,)),
            dma((2, CORES, nx, nz)),
            dma((2, nz)),
            dma((2, nx, nz)),
            dma((2, nx, nz)),
            dma((chunks,)),
            dma((chunks,)),
            dma((chunks, nx)),
            dma((chunks, nx)),
            dma((chunks, nz)),
            dma((chunks, nz)),
        ],
        compiler_params=pltpu.CompilerParams(
            collective_id=0, has_side_effects=True, vmem_limit_bytes=VMEM_LIMIT
        ),
        cost_estimate=pl.CostEstimate(
            flops=4 * DEPTHS * rows * features * width,
            bytes_accessed=6 * features * width,
            transcendentals=0,
        ),
    )(
        hidden0,
        embeds,
        parents,
        active,
        verify_row.reshape(1, 1),
        norm_gain.reshape(1, -1),
        norm_shift.reshape(1, -1),
        weight_in,
        bias_in.reshape(1, -1),
        weight_out,
        bias_out.reshape(1, -1),
    )


def solution(mesh):
    nz = mesh.shape["neuron"]
    nx = mesh.shape["req"] // CORES
    return jax.shard_map(
        functools.partial(body, nz, nx),
        mesh=mesh,
        in_specs=(
            P(("groups", "neuron", "req"), None, None),
            P(None, ("groups", "neuron", "req"), None, None),
            P(None, ("groups", "neuron", "req"), None),
            P(None, ("groups", "neuron", "req"), None, None),
            P(("groups", "neuron", "req")),
            P(),
            P(),
            P(None, ("neuron", "req")),
            P(("neuron", "req")),
            P(("neuron", "req"), None),
            P(),
        ),
        out_specs=(
            P(("groups", "neuron", "req"), None, None),
            P(("groups", "neuron", "req"), None),
        ),
        check_vma=False,
    )
```

```python
import functools

import jax
import jax.numpy as jnp
from jax import lax
from jax.experimental import pallas as pl
from jax.experimental.pallas import tpu as pltpu
from jax.sharding import PartitionSpec as P

BS = 128
DEPTHS = 2
CORES = 2
CHUNK = 1024
SUB = CHUNK // 2
SLOTS = 4
LAGS = (1, 3, 5)
PARTS = 2
ROWS = 8
VMEM_LIMIT = 63 * 1024 * 1024

norm_eps = 1e-05
MESH = pl.DeviceIdType.MESH
F32 = jnp.float32
BF16 = jnp.bfloat16


def kernel(
    nz,
    nx,
    hidden_ref,
    embeds_ref,
    parents_ref,
    active_ref,
    vrow_ref,
    gain_ref,
    shift_ref,
    win_hbm,
    bin_ref,
    wout_hbm,
    bout_ref,
    draft_ref,
    verified_ref,
    win_v,
    wout_v,
    xbuf,
    mbuf,
    mask_v,
    flag_v,
    acc,
    hid,
    ybuf,
    rc,
    rx,
    rz,
    pre_v,
    state_v,
    ver_v,
    vline,
    win_sem,
    wout_sem,
    ag_zr,
    ag_xr,
    ag_cr,
    ag_zs,
    ag_xs,
    ag_cs,
    rc_send,
    rc_recv,
    rx_send,
    rx_recv,
    rz_send,
    rz_recv,
):
    shards = CORES * nx * nz
    features = hidden_ref.shape[2]
    part = features // PARTS
    half = part // 2
    tiles, _, ht = acc.shape
    nblk = mask_v.shape[1]
    blk_tile = ht // BS
    chunks = features // CHUNK
    outs_dev = features // SUB
    all_rows = shards * ROWS

    g = lax.axis_index("groups")
    z = lax.axis_index("neuron")
    req = lax.axis_index("req")
    x = req // CORES
    c = req % CORES
    me = z * (nx * CORES) + req
    oc = 1 - c

    def dev(zz, xx, cc):
        return (g, zz, xx * CORES + cc)

    def zpeer(d):
        out, bit = z, 1
        while bit < nz:
            if d & bit:
                out = out + bit - 2 * bit * ((z // bit) % 2)
            bit *= 2
        return out

    zs = [zpeer(d) for d in range(nz)]
    xs = [(x + e) % nx for e in range(nx)]

    barrier = pltpu.get_barrier_semaphore()
    peers = [dev(zs[d], x, c) for d in range(1, nz)]
    peers += [dev(z, xs[e], c) for e in range(1, nx)]
    peers += [dev(z, x, oc)]
    for peer in peers:
        pl.semaphore_signal(barrier, inc=1, device_id=peer, device_id_type=MESH)

    def win_copy(a):
        return pltpu.make_async_copy(
            win_hbm.at[pl.ds(a * part, part), :], win_v.at[a], win_sem.at[a]
        )

    def wout_copy(k):
        col = pl.multiple_of((k % outs_dev) * SUB, SUB)
        slot = k % SLOTS
        return pltpu.make_async_copy(
            wout_hbm.at[:, pl.ds(col, SUB)], wout_v.at[slot], wout_sem.at[slot]
        )

    for a in range(PARTS):
        win_copy(a).start()
    for k in range(SLOTS):
        wout_copy(k).start()

    block_ids = lax.broadcasted_iota(jnp.int32, (ROWS, nblk), 1)
    row_ids = lax.broadcasted_iota(jnp.int32, (ROWS, BS), 0)
    flag = (row_ids == vrow_ref[...]).astype(F32)
    sides = []
    for depth in range(DEPTHS):
        listed = active_ref[depth, 0]
        member = jnp.zeros((ROWS, nblk), F32)
        for j in range(listed.shape[1]):
            member = jnp.where(listed[:, j : j + 1] == block_ids, 1.0, member)
        sides.append(jnp.concatenate([member, flag], axis=1))
    mbuf[c, x, z] = jnp.concatenate(sides, axis=0).astype(BF16)

    def prepare(depth):
        states = hidden_ref[0].astype(F32) if depth == 0 else state_v[...]
        eye_r = lax.broadcasted_iota(jnp.int32, (ROWS, ROWS), 0)
        eye_c = lax.broadcasted_iota(jnp.int32, (ROWS, ROWS), 1)
        par = jnp.sum(
            jnp.where(eye_r == eye_c, jnp.broadcast_to(parents_ref[depth], (ROWS, ROWS)), 0),
            axis=1,
            keepdims=True,
        )
        picked = jnp.zeros((ROWS, features), F32)
        for p in range(ROWS):
            picked = jnp.where(par == p, states[p : p + 1, :], picked)
        pre = picked + embeds_ref[depth, 0].astype(F32)
        pre_v[...] = pre
        centered = pre - jnp.mean(pre, axis=-1, keepdims=True)
        var = jnp.mean(centered * centered, axis=-1, keepdims=True)
        normed = centered * lax.rsqrt(var + norm_eps) * gain_ref[...] + shift_ref[...]
        for a in range(PARTS):
            two = [normed[:, a * part + h * half : a * part + (h + 1) * half] for h in range(2)]
            xbuf[a, c, x, z] = jnp.concatenate(two, axis=0).astype(BF16)

    def gather_steps(depth):
        started = [[] for _ in range(PARTS)]

        def refs(a):
            pairs = [(a + 1, xbuf.at[a])]
            return [(0, mbuf)] + pairs if depth == 0 and a == 0 else pairs

        def send(a, ref, to, send_sem, recv_sem):
            copy = pltpu.make_async_remote_copy(
                src_ref=ref,
                dst_ref=ref,
                send_sem=send_sem,
                recv_sem=recv_sem,
                device_id=to,
                device_id_type=MESH,
            )
            copy.start()
            started[a].append(copy)

        def arrived(ref, sem):
            pltpu.make_async_copy(ref, ref, sem).wait()

        def x_send(a, d):
            for b, buf in refs(a):
                for e in range(1, nx):
                    block = buf.at[c, x, zs[d]]
                    send(a, block, dev(z, xs[e], c), ag_xs.at[b, e, d], ag_xr.at[b, x, zs[d]])

        def own(a):
            for b, buf in refs(a):
                for d in range(1, nz):
                    send(a, buf.at[c, x, z], dev(zs[d], x, c), ag_zs.at[b, d], ag_zr.at[b, z])
            x_send(a, 0)

        def along_x(a):
            for d in range(1, nz):
                for b, buf in refs(a):
                    arrived(buf.at[c, x, zs[d]], ag_zr.at[b, zs[d]])
                x_send(a, d)
            for b, buf in refs(a):
                send(a, buf.at[c, x], dev(z, x, oc), ag_cs.at[b, 0], ag_cr.at[b, x])

        def along_core(a):
            for e in range(1, nx):
                for b, buf in refs(a):
                    for d in range(nz):
                        arrived(buf.at[c, xs[e], zs[d]], ag_xr.at[b, xs[e], zs[d]])
                    send(a, buf.at[c, xs[e]], dev(z, x, oc), ag_cs.at[b, e], ag_cr.at[b, xs[e]])

        def finish(a):
            for e in range(nx):
                for b, buf in refs(a):
                    arrived(buf.at[oc, xs[e]], ag_cr.at[b, xs[e]])
            for copy in started[a]:
                copy.wait_send()
            swap_rows(a)

        return own, along_x, along_core, finish

    def swap_rows(a):
        @pl.loop(0, CORES * nx)
        def _(i):
            cc, xx = i // nx, i % nx
            for zz in range(0, nz, 2):
                first = xbuf[a, cc, xx, zz].astype(F32)
                second = xbuf[a, cc, xx, zz + 1].astype(F32)
                xbuf[a, cc, xx, zz] = jnp.concatenate([first[:ROWS], second[:ROWS]], axis=0).astype(BF16)
                xbuf[a, cc, xx, zz + 1] = jnp.concatenate([first[ROWS:], second[ROWS:]], axis=0).astype(BF16)

    def read_flags(depth):
        meta = mbuf[...].astype(F32).reshape(shards, DEPTHS * ROWS, nblk + BS)
        meta = meta[:, depth * ROWS : (depth + 1) * ROWS, :].reshape(all_rows, nblk + BS)
        mask_v[...] = meta[:, :nblk].astype(BF16)
        if depth == DEPTHS - 1:
            flag_v[...] = meta[:, nblk:]

    def first_projection(depth, a):
        if depth == 0:
            win_copy(a).wait()

        @pl.loop(0, tiles)
        def _(t):
            col = pl.ds(pl.multiple_of(t * ht, ht), ht)
            pairs = xbuf.reshape(PARTS, shards // 2, 2, 2 * ROWS, half)
            pre = jnp.dot(
                pairs[a, :, 0].reshape(all_rows, half), win_v[a, :half, col], preferred_element_type=F32
            )
            pre += jnp.dot(
                pairs[a, :, 1].reshape(all_rows, half), win_v[a, half:, col], preferred_element_type=F32
            )
            if a > 0:
                pre += acc[t]
            if a < PARTS - 1:
                acc[t] = pre
                return
            act = jnp.maximum(pre + bin_ref[:, col], 0.0)
            which = lax.broadcasted_iota(jnp.int32, (nblk, ht), 0)
            unit = lax.broadcasted_iota(jnp.int32, (nblk, ht), 1) // BS
            spread = (which == unit + (me * tiles + t) * blk_tile).astype(F32).astype(BF16)
            keep = jnp.dot(mask_v[...], spread, preferred_element_type=F32)
            hid[:all_rows, col] = (act * keep).astype(BF16)
            if depth == DEPTHS - 1:
                wide = jnp.concatenate([flag_v[...]] * blk_tile, axis=1)
                one = jnp.sum((act * wide).reshape(shards, ROWS, ht), axis=1)
                hid[all_rows:, col] = one.astype(BF16)

    def second_projection(depth):
        last = depth == DEPTHS - 1
        width = SUB + BS if last else SUB
        lanes = pl.ds(0, width)
        rows = hid.shape[0] if last else all_rows

        def core_copy(n):
            return pltpu.make_async_remote_copy(
                src_ref=ybuf.at[n, oc, :, :, :, lanes],
                dst_ref=rc.at[n, :, :, :, lanes],
                send_sem=rc_send.at[n],
                recv_sem=rc_recv.at[n],
                device_id=dev(z, x, oc),
                device_id_type=MESH,
            )

        def x_copy(n, e):
            return pltpu.make_async_remote_copy(
                src_ref=ybuf.at[n, c, xs[e], :, :, lanes],
                dst_ref=rx.at[n, e - 1, :, :, lanes],
                send_sem=rx_send.at[n, e],
                recv_sem=rx_recv.at[n, e],
                device_id=dev(z, xs[e], c),
                device_id_type=MESH,
            )

        def z_copy(n, d):
            return pltpu.make_async_remote_copy(
                src_ref=ybuf.at[n, c, x, zs[d], :, lanes],
                dst_ref=rz.at[n, d - 1, :, lanes],
                send_sem=rz_send.at[n, d],
                recv_sem=rz_recv.at[n, d],
                device_id=dev(zs[d], x, c),
                device_id_type=MESH,
            )

        def compute(n):
            slot = []
            for sub in range(2):
                k = depth * outs_dev + n * 2 + sub
                wout_copy(k).wait()
                slot.append(k % SLOTS)
            pieces = jnp.zeros((shards, ROWS, BS), F32)
            place = lax.broadcasted_iota(jnp.int32, (shards, ROWS, BS), 1)
            step = 256
            for q in range(SUB // step):
                cols = slice(q * step, (q + 1) * step)
                parts = []
                for sub in range(2):
                    y = jnp.dot(hid[:rows, :], wout_v[slot[sub], :, cols], preferred_element_type=F32)
                    parts.append(y[:all_rows].reshape(shards, ROWS, step))
                    if last:
                        for r in range(step // BS):
                            spot = (sub * SUB + q * step) // BS + r
                            line = y[all_rows : all_rows + shards, r * BS : (r + 1) * BS]
                            pieces = jnp.where(place == spot, line[:, None, :], pieces)
                packed = jnp.concatenate(parts, axis=1).astype(BF16)
                ybuf[n, :, :, :, :, cols] = packed.reshape(CORES, nx, nz, 2 * ROWS, step)
            if last:
                packed = jnp.concatenate([pieces, jnp.zeros_like(pieces)], axis=1).astype(BF16)
                ybuf[n, :, :, :, :, SUB:] = packed.reshape(CORES, nx, nz, 2 * ROWS, BS)
            core_copy(n).start()
            for sub in range(2):
                k = depth * outs_dev + n * 2 + sub + SLOTS

                @pl.when(k < DEPTHS * outs_dev)
                def _():
                    wout_copy(k).start()

        def add_core(n):
            core_copy(n).wait_recv()
            for xx in range(nx):
                total = ybuf[n, c, xx, :, :, :width].astype(F32) + rc[n, xx, :, :, :width].astype(F32)
                ybuf[n, c, xx, :, :, :width] = total.astype(BF16)
            for e in range(1, nx):
                x_copy(n, e).start()

        def add_x(n):
            total = ybuf[n, c, x, :, :, :width].astype(F32)
            for e in range(1, nx):
                x_copy(n, e).wait_recv()
                total += rx[n, e - 1, :, :, :width].astype(F32)
            ybuf[n, c, x, :, :, :width] = total.astype(BF16)
            for d in range(1, nz):
                z_copy(n, d).start()

        def add_z(n):
            total = ybuf[n, c, x, z, :, :width].astype(F32)
            for d in range(1, nz):
                z_copy(n, d).wait_recv()
                total += rz[n, d - 1, :, :width].astype(F32)
            cols = pl.ds(pl.multiple_of(n * CHUNK, CHUNK), CHUNK)
            rows_out = jnp.concatenate([total[:ROWS, :SUB], total[ROWS:, :SUB]], axis=1)
            state_v[:, cols] = pre_v[:, cols] + (rows_out + bout_ref[:, cols])
            if last:
                ver_v[n] = total[:ROWS, SUB:]

        @pl.loop(0, chunks + LAGS[-1])
        def _(n):
            @pl.when(n < chunks)
            def _():
                compute(n)

            for lag, stage in zip(LAGS, (add_core, add_x, add_z)):

                @pl.when((n >= lag) & (n < chunks + lag))
                def _():
                    stage(n - lag)

        @pl.loop(0, chunks)
        def _(n):
            core_copy(n).wait_send()
            for e in range(1, nx):
                x_copy(n, e).wait_send()
            for d in range(1, nz):
                z_copy(n, d).wait_send()

    prepare(0)
    pl.semaphore_wait(barrier, len(peers))
    for depth in range(DEPTHS):
        if depth > 0:
            prepare(depth)
        own, along_x, along_core, finish = gather_steps(depth)
        for a in range(PARTS):
            own(a)
        along_x(0)
        along_core(0)
        for a in range(PARTS):
            if a + 1 < PARTS:
                along_x(a + 1)
            finish(a)
            if a == 0:
                read_flags(depth)
            first_projection(depth, a)
            if a + 1 < PARTS:
                along_core(a + 1)
        second_projection(depth)

    draft_ref[0] = state_v[...].astype(BF16)
    full_ids = lax.broadcasted_iota(jnp.int32, (ROWS, features), 0)
    base = jnp.sum(jnp.where(full_ids == vrow_ref[...], pre_v[...], 0.0), axis=0, keepdims=True)
    for n in range(chunks):
        piece = ver_v[n]
        for r in range(ROWS):
            vline[:, n * CHUNK + r * BS : n * CHUNK + (r + 1) * BS] = piece[r : r + 1, :]
    verified_ref[...] = (base + bout_ref[...] + vline[...]).astype(BF16)


def tile_width(width, most):
    return max(t for t in range(BS, most + 1, BS) if width % t == 0)


def body(
    nz,
    nx,
    hidden0,
    embeds,
    parents,
    active,
    verify_row,
    norm_gain,
    norm_shift,
    weight_in,
    bias_in,
    weight_out,
    bias_out,
):
    features, width = weight_in.shape
    shards = CORES * nx * nz
    rows = shards * ROWS
    nblk = shards * width // BS
    ht = tile_width(width, 512)
    tiles = width // ht
    chunks = features // CHUNK
    vm = pl.BlockSpec(memory_space=pltpu.VMEM)
    hbm = pl.BlockSpec(memory_space=pl.ANY)
    dma = pltpu.SemaphoreType.DMA
    return pl.pallas_call(
        functools.partial(kernel, nz, nx),
        out_shape=(
            jax.ShapeDtypeStruct(hidden0.shape, BF16),
            jax.ShapeDtypeStruct((1, features), BF16),
        ),
        in_specs=[vm, vm, vm, vm, vm, vm, vm, hbm, vm, hbm, vm],
        out_specs=(vm, vm),
        scratch_shapes=[
            pltpu.VMEM((PARTS, features // PARTS, width), BF16),
            pltpu.VMEM((SLOTS, width, SUB), BF16),
            pltpu.VMEM((PARTS, CORES, nx, nz, 2 * ROWS, features // PARTS // 2), BF16),
            pltpu.VMEM((CORES, nx, nz, DEPTHS * ROWS, nblk + BS), BF16),
            pltpu.VMEM((rows, nblk), BF16),
            pltpu.VMEM((rows, BS), F32),
            pltpu.VMEM((tiles, rows, ht), F32),
            pltpu.VMEM((rows + shards, width), BF16),
            pltpu.VMEM((chunks, CORES, nx, nz, 2 * ROWS, SUB + BS), BF16),
            pltpu.VMEM((chunks, nx, nz, 2 * ROWS, SUB + BS), BF16),
            pltpu.VMEM((chunks, nx - 1, nz, 2 * ROWS, SUB + BS), BF16),
            pltpu.VMEM((chunks, nz - 1, 2 * ROWS, SUB + BS), BF16),
            pltpu.VMEM((ROWS, features), F32),
            pltpu.VMEM((ROWS, features), F32),
            pltpu.VMEM((chunks, ROWS, BS), F32),
            pltpu.VMEM((1, features), F32),
            dma((PARTS,)),
            dma((SLOTS,)),
            dma((PARTS + 1, nz)),
            dma((PARTS + 1, nx, nz)),
            dma((PARTS + 1, nx)),
            dma((PARTS + 1, nz)),
            dma((PARTS + 1, nx, nz)),
            dma((PARTS + 1, nx)),
            dma((chunks,)),
            dma((chunks,)),
            dma((chunks, nx)),
            dma((chunks, nx)),
            dma((chunks, nz)),
            dma((chunks, nz)),
        ],
        compiler_params=pltpu.CompilerParams(
            collective_id=0, has_side_effects=True, vmem_limit_bytes=VMEM_LIMIT
        ),
        cost_estimate=pl.CostEstimate(
            flops=4 * DEPTHS * rows * features * width,
            bytes_accessed=6 * features * width,
            transcendentals=0,
        ),
    )(
        hidden0,
        embeds,
        parents,
        active,
        verify_row.reshape(1, 1),
        norm_gain.reshape(1, -1),
        norm_shift.reshape(1, -1),
        weight_in,
        bias_in.reshape(1, -1),
        weight_out,
        bias_out.reshape(1, -1),
    )


def solution(mesh):
    nz = mesh.shape["neuron"]
    nx = mesh.shape["req"] // CORES
    return jax.shard_map(
        functools.partial(body, nz, nx),
        mesh=mesh,
        in_specs=(
            P(("groups", "neuron", "req"), None, None),
            P(None, ("groups", "neuron", "req"), None, None),
            P(None, ("groups", "neuron", "req"), None),
            P(None, ("groups", "neuron", "req"), None, None),
            P(("groups", "neuron", "req")),
            P(),
            P(),
            P(None, ("neuron", "req")),
            P(("neuron", "req")),
            P(("neuron", "req"), None),
            P(),
        ),
        out_specs=(
            P(("groups", "neuron", "req"), None, None),
            P(("groups", "neuron", "req"), None),
        ),
        check_vma=False,
    )
```
